512 devices in a mesh: ex: 16 (over y, z_hi), par: 32 (over x, z_lo, core).
Axes of the slice: x: 4, y: 4, z: 16 (z_hi: 4, z_lo: 4; z = z_hi * 4 + z_lo), core: 2. Of those that a mesh axis runs over, the one named last changes fastest.
Arguments:
- normed_hidden_input: bfloat16 [64, 128, 4096], P('ex', None, 'par'), may hold values from -6 to 6
- attention_output: bfloat16 [64, 128, 4096], P('ex', None, 'par'), may hold values from -6 to 6
- query_output_gradient: bfloat16 [64, 128, 4096], P('ex', None, 'par'), may hold values from -6 to 6
- key_output_gradient: bfloat16 [64, 128, 4096], P('ex', None, 'par'), may hold values from -6 to 6
- value_output_gradient: bfloat16 [64, 128, 4096], P('ex', None, 'par'), may hold values from -6 to 6
- out_projection_gradient: bfloat16 [64, 128, 4096], P('ex', None, 'par'), may hold values from -6 to 6
- adapter_down_weight: bfloat16 [4, 128, 4096], P(None, 'ex', 'par'), may hold values from -0.09375 to 0.09375
- adapter_up_weight: bfloat16 [4, 4096, 128], P(None, 'par', 'ex'), may hold values from -0.09375 to 0.09375
- up_left_factor: bfloat16 [4, 4096, 64], P(None, 'par'), may hold values from -0.09375 to 0.09375
- up_right_factor: bfloat16 [4, 128, 128], replicated, may hold values from -0.5 to 0.5
- down_left_factor: bfloat16 [4, 128, 64], replicated, may hold values from -0.5 to 0.5
- down_right_factor: bfloat16 [4, 4096, 128], P(None, 'par'), may hold values from -0.09375 to 0.09375
Outputs:
- features: float32 [64, 8192], P('ex', 'par')
The draws below stay inside these ranges and needn't reach their ends.
All inputs are finite; a program needn't handle non-finite values.
Results may differ from the reference program's by a relative error of at most 0.005.
Values may be sent and summed in bfloat16 or wider, within the bound.
No kernel may reach another device: no remote copies, remote signals or barrier semaphores. Data moves between devices by JAX's collectives and lax.ppermute only.
A program may use at most 64 MiB of HBM per device.

```python
import jax
import jax.numpy as jnp
from jax import lax

MODEL_WIDTH = 4096
ADAPTER_RANK = 128
K1 = 64
K2 = 128
TOK_EX = 128
EXAMPLES = 64


def level_of(own_key, extent, cuts, smallest, largest):
    level = 1.0
    for axis_at, blocks in cuts:
        draws = jax.random.uniform(jax.random.fold_in(jax.random.fold_in(own_key, 6), axis_at), (blocks,), jnp.float32, smallest / len(cuts), largest / len(cuts))
        level = level * jnp.repeat(jnp.exp(draws), extent[axis_at] // blocks).reshape((-1,) + (1,) * (len(extent) - 1 - axis_at))
    return level


def gaussian(stream_key, extent, spread, reach, split=(), dtype=jnp.bfloat16):
    result = jax.random.normal(stream_key, extent, jnp.float32) * spread
    if len(split) > 0:
        result = level_of(stream_key, extent, split, -0.22, 0.18) * result
    return jnp.clip(result, min=-reach, max=reach).astype(dtype)


def setup_inputs(seed: int = 0) -> dict:
    key_of = jax.random.split(jax.random.key(seed), 13)
    return {
        "normed_hidden_input": gaussian(key_of[0], (EXAMPLES, TOK_EX, MODEL_WIDTH), 1.0, 6.0, ((0, 16), (2, 32))),
        "attention_output": gaussian(key_of[1], (EXAMPLES, TOK_EX, MODEL_WIDTH), 1.0, 6.0, ((0, 16), (2, 32))),
        "query_output_gradient": gaussian(key_of[2], (EXAMPLES, TOK_EX, MODEL_WIDTH), 1.0, 6.0, ((0, 16), (2, 32))),
        "key_output_gradient": gaussian(key_of[3], (EXAMPLES, TOK_EX, MODEL_WIDTH), 1.0, 6.0, ((0, 16), (2, 32))),
        "value_output_gradient": gaussian(key_of[4], (EXAMPLES, TOK_EX, MODEL_WIDTH), 1.0, 6.0, ((0, 16), (2, 32))),
        "out_projection_gradient": gaussian(key_of[5], (EXAMPLES, TOK_EX, MODEL_WIDTH), 1.0, 6.0, ((0, 16), (2, 32))),
        "adapter_down_weight": gaussian(key_of[6], (4, ADAPTER_RANK, MODEL_WIDTH), MODEL_WIDTH ** -0.5, 0.09375, ((1, 16), (2, 32))),
        "adapter_up_weight": gaussian(key_of[7], (4, MODEL_WIDTH, ADAPTER_RANK), MODEL_WIDTH ** -0.5, 0.09375, ((1, 32), (2, 16))),
        "up_left_factor": gaussian(key_of[8], (4, MODEL_WIDTH, K1), MODEL_WIDTH ** -0.5, 0.09375, ((1, 32),)),
        "up_right_factor": gaussian(key_of[9], (4, ADAPTER_RANK, K2), ADAPTER_RANK ** -0.5, 0.5),
        "down_left_factor": gaussian(key_of[10], (4, ADAPTER_RANK, K1), ADAPTER_RANK ** -0.5, 0.5),
        "down_right_factor": gaussian(key_of[11], (4, MODEL_WIDTH, K2), MODEL_WIDTH ** -0.5, 0.09375, ((1, 32),)),
    }


def block_sum(rows_in, weight):
    return jnp.dot(rows_in, weight, preferred_element_type=jnp.float32).astype(jnp.bfloat16)


def reference(normed_hidden_input, attention_output, query_output_gradient, key_output_gradient, value_output_gradient, out_projection_gradient, adapter_down_weight, adapter_up_weight, up_left_factor, up_right_factor, down_left_factor, down_right_factor):
    input_side = jnp.einsum("oyt,oyj->otj", adapter_down_weight.astype(jnp.float32), up_right_factor.astype(jnp.float32)).astype(jnp.bfloat16)
    gradient_side = jnp.einsum("ibc,icl->ibl", adapter_up_weight.astype(jnp.float32), down_left_factor.astype(jnp.float32)).astype(jnp.bfloat16)
    w_x = jnp.concatenate([input_side, down_right_factor], axis=2)
    w_g = jnp.concatenate([up_left_factor, gradient_side], axis=2)

    def one_example(items):
        hidden_rows, attn_rows, gq_rows, gk_rows, gv_rows, go_rows = items
        sources = (hidden_rows, hidden_rows, hidden_rows, attn_rows)
        grad_rows = (gq_rows, gk_rows, gv_rows, go_rows)
        x_parts = jnp.stack([block_sum(sources[module_id], w_x[module_id]) for module_id in range(4)], axis=1)
        g_parts = jnp.stack([block_sum(grad_rows[module_id], w_g[module_id]) for module_id in range(4)], axis=1)
        x_pairs = x_parts.reshape(TOK_EX, 8, K2).astype(jnp.float32)
        g_pairs = g_parts.reshape(TOK_EX, 8, K1).astype(jnp.float32)
        raw = jnp.einsum("tbi,tbj->ij", g_pairs, x_pairs)
        return raw.reshape(K1 * K2) * (1.0 / TOK_EX)

    return lax.map(one_example, (normed_hidden_input, attention_output, query_output_gradient, key_output_gradient, value_output_gradient, out_projection_gradient))
```

```python
import jax
import jax.numpy as jnp
from jax import lax
from jax.sharding import PartitionSpec as P

BF = jnp.bfloat16
F32 = jnp.float32

CHIPS = [[2 * chip + core for chip in range(16)] for core in range(2)]
Z_HI = [[4 * y + z for z in range(4)] for y in range(4)]
Y = [[4 * y + z for y in range(4)] for z in range(4)]
PAIR = [(i, i ^ 1) for i in range(32)]


def mm(a, b):
    return jnp.dot(a, b, preferred_element_type=F32)


def spread(block, axis, groups):
    count = len(groups[0])
    copies = jnp.broadcast_to(block[None], (count,) + block.shape)
    return lax.all_to_all(copies, axis, 0, 0, tiled=True, axis_index_groups=groups)


def per_device(
    hidden,
    attn,
    grad_q,
    grad_k,
    grad_v,
    grad_o,
    adapter_down,
    adapter_up,
    up_left,
    up_right,
    down_left,
    down_right,
):
    core = lax.axis_index("par") % 2

    shard = jnp.concatenate(
        [adapter_down.reshape(32, 128), adapter_up.transpose(0, 2, 1).reshape(32, 128)]
    )
    along_z = spread(shard, "ex", Z_HI).reshape(256, 128)
    gathered = spread(along_z, "ex", Y).reshape(16, 2, 4, 8, 128)
    gathered = gathered.transpose(1, 2, 0, 3, 4).reshape(2, 4, 128, 128)
    side_x = jnp.einsum("orf,orj->ofj", gathered[0], up_right, preferred_element_type=F32)
    side_g = jnp.einsum("irf,irl->ifl", gathered[1], down_left, preferred_element_type=F32)
    side_x = side_x.astype(BF)
    side_g = side_g.astype(BF)
    side = jnp.concatenate(
        [
            side_x,
            jnp.concatenate([side_g[0], side_g[1]], axis=1)[None],
            jnp.concatenate([side_g[2], side_g[3]], axis=1)[None],
        ]
    )
    side_other = lax.ppermute(side, "par", PAIR)

    inputs = [hidden, attn, grad_q, grad_k, grad_v, grad_o]
    keep = [lax.dynamic_slice_in_dim(a, 2 * core, 2, 0) for a in inputs]
    send = [lax.dynamic_slice_in_dim(a, 2 - 2 * core, 2, 0) for a in inputs]
    ul = [
        jnp.concatenate([up_left[0], up_left[1]], axis=1)[None],
        jnp.concatenate([up_left[2], up_left[3]], axis=1)[None],
    ]
    other = lax.ppermute(jnp.concatenate(send + ul + [down_right]), "par", PAIR)
    rows = [
        jnp.concatenate([keep[k], other[2 * k : 2 * k + 2]], axis=2).reshape(256, 256)
        for k in range(6)
    ]
    h_rows, a_rows, g_rows = rows[0], rows[1], rows[2:]
    dr = jnp.concatenate([down_right, other[14:18]], axis=1)
    ul_all = jnp.concatenate([jnp.concatenate(ul), other[12:14]], axis=1)
    ul_of = [ul_all[m // 2][:, 64 * (m % 2) : 64 * (m % 2) + 64] for m in range(4)]

    x_right = [mm(h_rows, jnp.concatenate([dr[0], dr[1], dr[2]], axis=1)), mm(a_rows, dr[3])]
    g_left = [mm(g_rows[m], ul_of[m]) for m in range(4)]
    part = jnp.concatenate([p.astype(BF) for p in x_right + g_left], axis=1)
    pieces = lax.all_to_all(
        part.reshape(16, 16, 768), "par", 0, 0, tiled=True, axis_index_groups=CHIPS
    )
    total = jnp.sum(pieces.astype(F32), axis=0).astype(BF)
    full = spread(total, "par", CHIPS).reshape(2, 128, 768)

    sx = jnp.concatenate([side_x, side_other[:4]], axis=1)
    sg_all = jnp.concatenate([side[4:], side_other[4:]], axis=1)
    sg = [sg_all[m // 2][:, 64 * (m % 2) : 64 * (m % 2) + 64] for m in range(4)]
    x_left = jnp.concatenate(
        [mm(h_rows, jnp.concatenate([sx[0], sx[1], sx[2]], axis=1)), mm(a_rows, sx[3])], axis=1
    ).astype(BF)
    g_right = [mm(g_rows[m], sg[m]).astype(BF) for m in range(4)]
    x_all = jnp.concatenate(
        [x_left.reshape(2, 128, 4, 128), full[:, :, :512].reshape(2, 128, 4, 128)], axis=2
    )
    g_all = jnp.concatenate(
        [
            full[:, :, 512:].reshape(2, 128, 4, 64),
            jnp.stack(g_right, axis=1).reshape(2, 128, 4, 64),
        ],
        axis=2,
    )
    raw = jnp.einsum("etbi,etbj->eij", g_all, x_all, preferred_element_type=F32)
    out = raw.reshape(2, 32, 256).transpose(1, 0, 2)
    out = lax.all_to_all(out, "par", 0, 0, tiled=True)
    out = jnp.sum(out.reshape(16, 4, 256), axis=0)
    return out * (1.0 / 128)


def solution(mesh):
    in_specs = (P("ex", None, "par"),) * 6 + (
        P(None, "ex", "par"),
        P(None, "par", "ex"),
        P(None, "par", None),
        P(),
        P(),
        P(None, "par", None),
    )
    return jax.shard_map(
        per_device, mesh=mesh, in_specs=in_specs, out_specs=P("ex", "par"), check_vma=False
    )
```

```python
import jax
import jax.numpy as jnp
from jax import lax
from jax.experimental import pallas as pl
from jax.experimental.pallas import tpu as pltpu
from jax.sharding import PartitionSpec as P

BF = jnp.bfloat16
F32 = jnp.float32

CHIPS = [[2 * chip + core for chip in range(16)] for core in range(2)]
Z_HI = [[4 * y + z for z in range(4)] for y in range(4)]
Y = [[4 * y + z for y in range(4)] for z in range(4)]
PAIR = [(i, i ^ 1) for i in range(32)]
VMEM = pl.BlockSpec(memory_space=pltpu.VMEM)
HBM = pl.BlockSpec(memory_space=pl.ANY)


def call(kernel, outs, *operands, specs=None, scratch=()):
    specs = specs or [VMEM] * len(operands)
    operands = [
        pltpu.with_memory_space_constraint(a, pltpu.VMEM) if spec is VMEM else a
        for a, spec in zip(operands, specs)
    ]
    return pl.pallas_call(
        kernel,
        out_shape=tuple(pltpu.VMEM(shape, dtype) for shape, dtype in outs),
        in_specs=specs,
        out_specs=(VMEM,) * len(outs),
        scratch_shapes=scratch,
        name=kernel.__name__,
    )(*operands)


def dot(a, b, over_a, over_b):
    return lax.dot_general(a, b, (((over_a,), (over_b,)), ((), ())), preferred_element_type=F32)


def spread(block, axis, groups):
    count = len(groups[0])
    copies = jnp.broadcast_to(block[None], (count,) + block.shape)
    return lax.all_to_all(copies, axis, 0, 0, tiled=True, axis_index_groups=groups)


def pack_kernel(*refs):
    inputs, (down_right, up_left, send, keep, sem) = refs[:6], refs[6:]
    mine = 2 * lax.rem(lax.axis_index("par"), 2)
    copies = []
    for k in range(6):
        for first, to in ((2 - mine, send), (mine, keep)):
            copies.append((inputs[k].at[pl.ds(first, 2)], to.at[pl.ds(2 * k, 2)]))
    copies.append((up_left, send.at[pl.ds(12, 2)]))
    copies.append((down_right, send.at[pl.ds(14, 4)]))
    copies = [pltpu.make_async_copy(a, b, sem) for a, b in copies]
    for copy in copies:
        copy.start()
    for copy in copies:
        copy.wait()


def pack(inputs, down_right, up_left):
    return call(
        pack_kernel,
        [((18, 128, 128), BF), ((12, 128, 128), BF)],
        *inputs,
        down_right,
        up_left,
        specs=[HBM] * 8,
        scratch=[pltpu.SemaphoreType.DMA],
    )


def rows_of(keep, other, k):
    own = keep[2 * k : 2 * k + 2].reshape(256, 128)
    far = other[2 * k : 2 * k + 2].reshape(256, 128)
    return jnp.concatenate([own, far], axis=1)


def first_kernel(keep, down_right, up_left, other, part):
    def put(at, value):
        part[:, :, at : at + value.shape[1]] = value.astype(BF).reshape(16, 16, value.shape[1])

    weight = [jnp.concatenate([down_right[m], other[14 + m]], axis=0) for m in range(4)]
    hidden = rows_of(keep, other, 0)
    put(0, dot(hidden, jnp.concatenate(weight[:2], axis=1), 1, 0))
    put(256, dot(hidden, weight[2], 1, 0))
    put(384, dot(rows_of(keep, other, 1), weight[3], 1, 0))
    for half in range(2):
        weight = jnp.concatenate([up_left[half], other[12 + half]], axis=1)
        pair = [
            dot(rows_of(keep, other, 2 + 2 * half + i), weight[64 * i : 64 * i + 64], 1, 1)
            for i in range(2)
        ]
        put(512 + 128 * half, jnp.concatenate(pair, axis=1))


def first(keep, down_right, up_left, other):
    return call(first_kernel, [((16, 16, 768), BF)], keep, down_right, up_left, other)[0]


ORDER = (0, 1, 3, 2)


def side_kernel(near, next_y, far_y, factor, out):
    place = lax.axis_index("ex")
    start = [
        pl.multiple_of(16 * jnp.bitwise_xor(place, 4 * y + z), 16) for y in ORDER for z in ORDER
    ]
    for m in range(4):
        at = slice(16 * m, 16 * m + 16)
        ranks = jnp.concatenate(
            [b[:, at, :].reshape(-1, 128) for b in (near, next_y, far_y)], axis=0
        )
        rows = jnp.concatenate([factor[m, pl.ds(s, 16), :] for s in start], axis=0)
        side = dot(ranks, rows, 0, 0).astype(BF)
        out[m] = side[:, :128]
        out[4 + m // 2, :, 64 * (m % 2) : 64 * (m % 2) + 64] = side[:, 128:]


def side_weights(near, next_y, far_y, factor):
    return call(side_kernel, [((6, 128, 128), BF)], near, next_y, far_y, factor)[0]


def late_kernel(keep, other, side, side_other, x_part, g_part):
    for m in range(4):
        source = rows_of(keep, other, 0 if m < 3 else 1)
        weight = jnp.concatenate([side[m], side_other[m]], axis=0)
        x_part[m] = dot(weight, source, 0, 1).astype(BF)
    for half in range(2):
        weight = jnp.concatenate([side[4 + half], side_other[4 + half]], axis=0)
        for i in range(2):
            m = 2 * half + i
            value = dot(weight, rows_of(keep, other, 2 + m), 0, 1)
            g_part[m] = value[64 * i : 64 * i + 64].astype(BF)


def late(keep, other, side, side_other):
    return call(
        late_kernel, [((4, 128, 256), BF), ((4, 64, 256), BF)], keep, other, side, side_other
    )


def join_kernel(full, x_part, g_part, out):
    for e in range(2):
        at = slice(128 * e, 128 * e + 128)
        rows = full[8 * e : 8 * e + 8].reshape(128, 768)
        right = jnp.zeros((64, 128), F32)
        left = [jnp.zeros((128, 128), F32)] * 2
        for m in range(4):
            right += dot(g_part[m, :, at], rows[:, 128 * m : 128 * m + 128], 1, 0)
            both = rows[:, 512 + 128 * (m // 2) : 640 + 128 * (m // 2)]
            left[m % 2] += dot(x_part[m, :, at], both, 1, 0)
        total = right + left[0].T[:64] + left[1].T[64:]
        out[:, 2 * e : 2 * e + 2] = total.reshape(32, 2, 128)


def join(full, x_part, g_part):
    return call(join_kernel, [((32, 4, 128), F32)], full, x_part, g_part)[0]


def swap(block, step):
    return lax.ppermute(block, "ex", [(i, i ^ step) for i in range(16)])


def per_device(*args):
    inputs, (lora_a, lora_b, up_left, up_right, down_left, down_right) = args[:6], args[6:]

    shard = jnp.concatenate([lora_a, lora_b.transpose(0, 2, 1)], axis=1).reshape(64, 128)
    factor = jnp.concatenate(
        [
            jnp.pad(up_right.reshape(4, 16, 8, 128), ((0, 0), (0, 0), (0, 0), (0, 64))),
            jnp.pad(down_left.reshape(4, 16, 8, 64), ((0, 0), (0, 0), (0, 0), (128, 0))),
        ],
        axis=2,
    ).reshape(4, 256, 192)

    up_left = up_left.transpose(0, 2, 1).reshape(2, 128, 128)

    send, keep = pack(inputs, down_right, up_left)
    other = lax.ppermute(send, "par", PAIR)
    one = swap(shard[None], 1)
    part = first(keep, down_right, up_left, other)
    part, one = lax.optimization_barrier((part, one))
    pieces = lax.all_to_all(part, "par", 0, 0, tiled=True, axis_index_groups=CHIPS)
    two = jnp.concatenate([shard[None], one])
    near = jnp.concatenate([two, swap(two, 3)])
    next_y = swap(near, 4)
    total = jnp.sum(pieces.astype(F32), axis=0).astype(BF)
    total, near, next_y = lax.optimization_barrier((total, near, next_y))
    full = spread(total, "par", CHIPS)
    far_y = swap(jnp.concatenate([near, next_y]), 12)
    side = side_weights(near, next_y, far_y, factor)
    side_other = lax.ppermute(side, "par", PAIR)
    x_part, g_part = late(keep, other, side, side_other)
    out = join(full, x_part, g_part)

    out = lax.all_to_all(out, "par", 0, 0, tiled=True)
    out = jnp.sum(out.reshape(16, 4, 2, 128), axis=0) * (1.0 / 128)
    return out.reshape(4, 256)


def solution(mesh):
    in_specs = (P("ex", None, "par"),) * 6 + (
        P(None, "ex", "par"),
        P(None, "par", "ex"),
        P(None, "par", None),
        P(),
        P(),
        P(None, "par", None),
    )
    return jax.shard_map(
        per_device, mesh=mesh, in_specs=in_specs, out_specs=P("ex", "par"), check_vma=False
    )
```

```python
import jax
import jax.numpy as jnp
from jax import lax
from jax.experimental import pallas as pl
from jax.experimental.pallas import tpu as pltpu
from jax.sharding import PartitionSpec as P

BF = jnp.bfloat16
F32 = jnp.float32

Z_HI = [[4 * y + z for z in range(4)] for y in range(4)]
Y = [[4 * y + z for y in range(4)] for z in range(4)]
CHIPS = [[2 * chip + core for chip in range(16)] for core in range(2)]
PAIR = [(i, i ^ 1) for i in range(32)]
CHAIN = 0
VMEM = pl.BlockSpec(memory_space=pltpu.VMEM)
HBM = pl.BlockSpec(memory_space=pl.ANY)
LOOSE = pl.BlockSpec(memory_space=pltpu.VMEM)


def call(kernel, outs, *operands, specs=None, scratch=(), place=pltpu.VMEM):
    specs = specs or [VMEM] * len(operands)
    operands = [
        pltpu.with_memory_space_constraint(a, pltpu.VMEM) if spec is VMEM else a
        for a, spec in zip(operands, specs)
    ]
    return pl.pallas_call(
        kernel,
        out_shape=tuple(place(shape, dtype) for shape, dtype in outs),
        in_specs=specs,
        out_specs=(VMEM,) * len(outs),
        scratch_shapes=scratch,
        name=kernel.__name__,
    )(*operands)


def dot(a, b, over_a, over_b):
    return lax.dot_general(a, b, (((over_a,), (over_b,)), ((), ())), preferred_element_type=F32)


def spread(block, axis, groups):
    count = len(groups[0])
    copies = jnp.broadcast_to(block[None], (count,) + block.shape)
    return lax.all_to_all(copies, axis, 0, 0, tiled=True, axis_index_groups=groups)


UL, DR, RANKS, ALL = 3072, 3328, 3840, 3904


def pack_kernel(*refs):
    inputs, (down_right, up_left, lora_a, lora_b, send, ranks, sem) = refs[:6], refs[6:]
    copies = [(lora_a, ranks.at[0]), (lora_b, ranks.at[1])]
    copies += [(inputs[k], send.at[pl.ds(512 * k, 512)]) for k in range(6)]
    copies.append((up_left, send.at[pl.ds(UL, 256)]))
    copies.append((down_right, send.at[pl.ds(DR, 512)]))
    copies = [pltpu.make_async_copy(a, b, sem) for a, b in copies]
    for copy in copies:
        copy.start()
    for copy in copies:
        copy.wait()
    a, b = ranks[0].astype(F32), ranks[1].astype(F32)
    parts = [v[8 * m : 8 * m + 8] for m in range(4) for v in (a, b)]
    send[RANKS:ALL] = jnp.concatenate(parts, axis=0).astype(BF)


def pack(inputs, down_right, up_left, lora_a, lora_b):
    return call(
        pack_kernel,
        [((ALL, 128), BF)],
        *[a.reshape(512, 128) for a in inputs],
        down_right.reshape(512, 128),
        up_left.transpose(0, 2, 1).reshape(256, 128),
        lora_a.reshape(32, 128),
        lora_b.transpose(0, 2, 1).reshape(32, 128),
        specs=[HBM] * 10,
        scratch=[pltpu.VMEM((2, 32, 128), BF), pltpu.SemaphoreType.DMA],
    )[0]


def rows_of(own, other, k):
    at = slice(512 * k, 512 * k + 512)
    return jnp.concatenate([own[at], other[at]], axis=1)


def first_kernel(own, other, part, ranks, far):
    role = lax.rem(lax.axis_index("par") + CHAIN, 2)
    start = pl.multiple_of(256 * role, 256)
    ranks[:64] = own[RANKS:ALL]
    ranks[64:] = other[RANKS:ALL]
    for k in range(6):
        at = slice(256 * k, 256 * k + 256)
        far[at] = other[pl.ds(512 * k + start, 256)]

    def put(at, value):
        part[:, :, at : at + value.shape[1]] = value.astype(BF).reshape(16, 32, value.shape[1])

    def right(m):
        at = slice(DR + 128 * m, DR + 128 * m + 128)
        return jnp.concatenate([own[at], other[at]], axis=0)

    @pl.when(role == 0)
    def _():
        hidden = rows_of(own, other, 0)
        put(0, dot(hidden, jnp.concatenate([right(0), right(1)], axis=1), 1, 0))
        put(256, dot(hidden, right(2), 1, 0))
        put(384, dot(rows_of(own, other, 1), right(3), 1, 0))
        left = jnp.concatenate([own[UL:DR], other[UL:DR]], axis=1)
        for half in range(2):
            pair = [
                dot(rows_of(own, other, 2 + m), left[64 * m : 64 * m + 64], 1, 1)
                for m in (2 * half, 2 * half + 1)
            ]
            put(512 + 128 * half, jnp.concatenate(pair, axis=1))

    @pl.when(role == 1)
    def _():
        part[...] = jnp.zeros_like(part)


def first(own, other):
    rows = ((UL // 2, 128), BF)
    shapes = [((16, 32, 768), BF), ((128, 128), BF), rows]
    return call(first_kernel, shapes, own, other, place=jax.ShapeDtypeStruct)


def side_kernel(gathered, factor, out):
    for m in range(4):
        for core in range(2):
            at = slice(64 * core + 16 * m, 64 * core + 16 * m + 16)
            ranks = gathered[:, at, :].reshape(256, 128)
            side = dot(ranks, factor[m], 0, 0).astype(BF)
            rows = slice(128 - 128 * core, 256 - 128 * core)
            out[rows, 128 * m : 128 * m + 128] = side[:, :128]
            out[rows, 512 + 64 * m : 576 + 64 * m] = side[:, 128:]
    out[256:] = jnp.zeros((256, 768), BF)


def load_kernel(*refs):
    inputs, (other, mine, far, sem) = refs[:6], refs[6:]
    role = lax.rem(lax.axis_index("par") + CHAIN, 2)
    rows = pl.ds(pl.multiple_of(256 * role, 256), 256)
    copies = [(inputs[k].at[rows], mine.at[pl.ds(256 * k, 256)]) for k in range(6)]
    copies.append((other, far))
    copies = [pltpu.make_async_copy(a, b, sem) for a, b in copies]
    for copy in copies:
        copy.start()
    for copy in copies:
        copy.wait()


def load(inputs, other):
    shape = ((1536, 128), BF)
    return call(
        load_kernel,
        [shape, shape],
        *[a.reshape(512, 128) for a in inputs],
        other,
        specs=[HBM] * 7,
        scratch=[pltpu.SemaphoreType.DMA],
    )


def finish_kernel(have, got, *refs):
    inputs, (other, out, mine, far, sem) = refs[:6], refs[6:]
    role = lax.rem(lax.axis_index("par") + CHAIN, 2)
    rows = pl.ds(pl.multiple_of(256 * role, 256), 256)
    copies = [(inputs[k].at[rows], mine.at[pl.ds(256 * k, 256)]) for k in range(6)]
    copies.append((other, far))
    copies = [pltpu.make_async_copy(a, b, sem) for a, b in copies]
    for copy in copies:
        copy.start()
    for copy in copies:
        copy.wait()

    def add_up(full, side, first, own, other):
        def rows(k):
            at = slice(256 * k, 256 * k + 256)
            return jnp.concatenate([own[at], other[at]], axis=1)

        hidden = rows(0)
        x_left = [dot(hidden, side[:256, 128 * m : 128 * m + 128], 1, 0) for m in range(3)]
        x_left.append(dot(rows(1), side[:256, 384:512], 1, 0))
        g_right = [dot(rows(2 + m), side[:256, 512 + 64 * m : 576 + 64 * m], 1, 0) for m in range(4)]
        x_left = [x.astype(BF) for x in x_left]
        g_right = [g.astype(BF) for g in g_right]
        for e in range(2):
            at, here = slice(128 * e, 128 * e + 128), slice(first + 128 * e, first + 128 * e + 128)
            total = jnp.zeros((64, 128), F32)
            for m in range(4):
                x, g = slice(128 * m, 128 * m + 128), slice(512 + 64 * m, 576 + 64 * m)
                total += dot(full[here, g], x_left[m][at], 0, 0)
                total += dot(g_right[m][at], full[here, x], 0, 0)
            out[:, 2 * e : 2 * e + 2] = total.reshape(32, 2, 128)

    mover = lax.rem(lax.axis_index("par"), 2) == CHAIN

    @pl.when(mover)
    def _():
        add_up(have, got, 0, mine, far)

    @pl.when(jnp.logical_not(mover))
    def _():
        add_up(got, have, 256, far, mine)


def move_rows(part, ranks, factor):
    pieces = lax.all_to_all(part, "par", 0, 0, tiled=True, axis_index_groups=CHIPS)
    total = jnp.sum(pieces.astype(F32), axis=0).astype(BF)
    return spread(total, "par", CHIPS).reshape(512, 768)


def gather_ranks(part, ranks, factor):
    along_z = spread(ranks, "ex", Z_HI).reshape(512, 128)
    gathered = spread(along_z, "ex", Y).reshape(16, 128, 128)
    return call(side_kernel, [((512, 768), BF)], gathered, factor, specs=[VMEM, LOOSE])[0]


def per_device(*args):
    inputs, (lora_a, lora_b, up_left, up_right, down_left, down_right) = args[:6], args[6:]

    factor = jnp.concatenate(
        [
            jnp.pad(up_right.reshape(4, 16, 8, 128), ((0, 0), (0, 0), (0, 0), (0, 64))),
            jnp.pad(down_left.reshape(4, 16, 8, 64), ((0, 0), (0, 0), (0, 0), (128, 0))),
        ],
        axis=2,
    ).reshape(4, 256, 192)

    own = pack(inputs, down_right, up_left, lora_a, lora_b)
    other = lax.ppermute(own, "par", PAIR)
    part, ranks, far = first(own, other)
    mover = lax.axis_index("par") % 2 == CHAIN
    have = lax.cond(mover, move_rows, gather_ranks, part, ranks, factor)
    got = lax.ppermute(have, "par", PAIR)
    out = call(finish_kernel, [((32, 4, 128), F32)], have, got, *[a.reshape(512, 128) for a in inputs], far, specs=[VMEM, VMEM] + [HBM] * 7, scratch=[pltpu.VMEM((1536, 128), BF), pltpu.VMEM((1536, 128), BF), pltpu.SemaphoreType.DMA])[0]
    out = lax.all_to_all(out, "par", 0, 0, tiled=True)
    out = jnp.sum(out.reshape(16, 4, 2, 128), axis=0) * (1.0 / 128)
    return out.reshape(4, 256)


def solution(mesh):
    in_specs = (P("ex", None, "par"),) * 6 + (
        P(None, "ex", "par"),
        P(None, "par", "ex"),
        P(None, "par", None),
        P(),
        P(),
        P(None, "par", None),
    )
    return jax.shard_map(
        per_device, mesh=mesh, in_specs=in_specs, out_specs=P("ex", "par"), check_vma=False
    )
```

```python
import jax
import jax.numpy as jnp
from jax import lax
from jax.experimental import pallas as pl
from jax.experimental.pallas import tpu as pltpu
from jax.sharding import PartitionSpec as P

BF = jnp.bfloat16
F32 = jnp.float32

Z_HI = [[4 * y + z for z in range(4)] for y in range(4)]
Y = [[4 * y + z for y in range(4)] for z in range(4)]
CHIPS = [[2 * chip + core for chip in range(16)] for core in range(2)]
PAIR = [(i, i ^ 1) for i in range(32)]
CHAIN = 0
VMEM = pl.BlockSpec(memory_space=pltpu.VMEM)
HBM = pl.BlockSpec(memory_space=pl.ANY)
LOOSE = pl.BlockSpec(memory_space=pltpu.VMEM)


def call(kernel, outs, *operands, specs=None, scratch=(), place=pltpu.VMEM, out_specs=None):
    specs = specs or [VMEM] * len(operands)
    operands = [
        pltpu.with_memory_space_constraint(a, pltpu.VMEM) if spec is VMEM else a
        for a, spec in zip(operands, specs)
    ]
    return pl.pallas_call(
        kernel,
        out_shape=tuple(place(shape, dtype) for shape, dtype in outs),
        in_specs=specs,
        out_specs=out_specs or (VMEM,) * len(outs),
        scratch_shapes=scratch,
        name=kernel.__name__,
    )(*operands)


def dot(a, b, over_a, over_b):
    return lax.dot_general(a, b, (((over_a,), (over_b,)), ((), ())), preferred_element_type=F32)


def spread(block, axis, groups):
    count = len(groups[0])
    copies = jnp.broadcast_to(block[None], (count,) + block.shape)
    return lax.all_to_all(copies, axis, 0, 0, tiled=True, axis_index_groups=groups)


UL, DR, RANKS, ALL = 3072, 3328, 3840, 3904


def pack_kernel(*refs):
    inputs, (down_right, up_left, lora_a, lora_b, send, ranks, sem) = refs[:6], refs[6:]
    copies = [(lora_a, ranks.at[0]), (lora_b, ranks.at[1])]
    copies += [(inputs[k], send.at[pl.ds(512 * k, 512)]) for k in range(6)]
    copies.append((up_left, send.at[pl.ds(UL, 256)]))
    copies.append((down_right, send.at[pl.ds(DR, 512)]))
    copies = [pltpu.make_async_copy(a, b, sem) for a, b in copies]
    for copy in copies:
        copy.start()
    for copy in copies:
        copy.wait()
    a, b = ranks[0].astype(F32), ranks[1].astype(F32)
    parts = [v[8 * m : 8 * m + 8] for m in range(4) for v in (a, b)]
    send[RANKS:ALL] = jnp.concatenate(parts, axis=0).astype(BF)


def pack(inputs, down_right, up_left, lora_a, lora_b):
    return call(
        pack_kernel,
        [((ALL, 128), BF)],
        *[a.reshape(512, 128) for a in inputs],
        down_right.reshape(512, 128),
        up_left.transpose(0, 2, 1).reshape(256, 128),
        lora_a.reshape(32, 128),
        lora_b.transpose(0, 2, 1).reshape(32, 128),
        specs=[HBM] * 10,
        scratch=[pltpu.VMEM((2, 32, 128), BF), pltpu.SemaphoreType.DMA],
    )[0]


def rows_of(own, other, k):
    at = slice(512 * k, 512 * k + 512)
    return jnp.concatenate([own[at], other[at]], axis=1)


def pick(rows, half, weight, over):
    low, high = [dot(rows(2 + 2 * half + i), weight, 1, over) for i in range(2)]
    return jnp.where(lax.broadcasted_iota(jnp.int32, low.shape, 1) < 64, low, high)


def first_kernel(own, other, part, ranks, far, sem):
    role = lax.rem(lax.axis_index("par") + CHAIN, 2)
    ranks[:64] = own[RANKS:ALL]
    ranks[64:] = other[RANKS:ALL]

    def put(at, value):
        part[:, :, at : at + value.shape[1]] = value.astype(BF).reshape(16, 32, value.shape[1])

    def right(m):
        at = slice(DR + 128 * m, DR + 128 * m + 128)
        return jnp.concatenate([own[at], other[at]], axis=0)

    @pl.when(role == 0)
    def _():
        hidden = rows_of(own, other, 0)
        put(0, dot(hidden, jnp.concatenate([right(0), right(1)], axis=1), 1, 0))
        put(256, dot(hidden, right(2), 1, 0))
        put(384, dot(rows_of(own, other, 1), right(3), 1, 0))
        left = jnp.concatenate([own[UL:DR], other[UL:DR]], axis=1)
        for half in range(2):
            weight = left[128 * half : 128 * half + 128]
            put(512 + 128 * half, pick(lambda k: rows_of(own, other, k), half, weight, 1))

    @pl.when(role == 1)
    def _():
        copy = pltpu.make_async_copy(other.at[pl.ds(0, UL)], far, sem)
        copy.start()
        copy.wait()


def first(own, other):
    shapes = [((16, 32, 768), BF), ((128, 128), BF), ((UL, 128), BF)]
    return call(
        first_kernel,
        shapes,
        own,
        other,
        scratch=[pltpu.SemaphoreType.DMA],
        place=jax.ShapeDtypeStruct,
        out_specs=(VMEM, VMEM, HBM),
    )


def parts_kernel(gathered, up_right, down_left, *refs):
    inputs, (far, keep, send) = refs[:6], refs[6:]
    nothing = jnp.zeros((16, 8, 128), F32)
    left_half = lax.broadcasted_iota(jnp.int32, (128, 128), 1) < 64
    side = [[], []]
    for m in range(4):
        pair = down_left[m // 2].astype(F32).T
        for_b = jnp.where(left_half if m % 2 == 0 else ~left_half, pair, 0.0)
        for_a = up_right[m].astype(F32)
        factor = jnp.concatenate(
            [
                jnp.concatenate([for_a.reshape(16, 8, 128), nothing], axis=1).reshape(256, 128),
                jnp.concatenate([nothing, for_b.reshape(16, 8, 128)], axis=1).reshape(256, 128),
            ],
            axis=1,
        ).astype(BF)
        for core in range(2):
            at = slice(64 * core + 16 * m, 64 * core + 16 * m + 16)
            ranks = gathered[:, at, :].reshape(256, 128)
            side[core].append(dot(ranks, factor, 0, 0).astype(BF))

    def weight(at, *modules):
        halves = [jnp.concatenate([half[m][:, at] for m in modules], axis=1) for half in side]
        return jnp.concatenate(halves, axis=0)

    def put(at, value):
        send[:, at : at + value.shape[1]] = value[:256].astype(BF)
        keep[:, at : at + value.shape[1]] = value[256:].astype(BF)

    x_at, g_at = slice(0, 128), slice(128, 256)
    def rows(k):
        return jnp.concatenate([inputs[k][...], far[512 * k : 512 * k + 512]], axis=1)

    hidden = rows(0)
    put(0, dot(hidden, weight(x_at, 0, 1), 1, 0))
    put(256, dot(hidden, weight(x_at, 2), 1, 0))
    put(384, dot(rows(1), weight(x_at, 3), 1, 0))
    for half in range(2):
        pair = weight(g_at, 2 * half) + weight(g_at, 2 * half + 1)
        put(512 + 128 * half, pick(rows, half, pair, 0))


def parts(gathered, up_right, down_left, inputs, other):
    return call(
        parts_kernel,
        [((256, 768), BF)] * 2,
        gathered,
        up_right,
        down_left,
        *inputs,
        other,
        specs=[VMEM, LOOSE, LOOSE] + [VMEM] * 7,
        place=jax.ShapeDtypeStruct,
    )


def join_kernel(keep, got, out):
    def add_up(full, parts):
        for e in range(2):
            at = slice(128 * e, 128 * e + 128)
            total = jnp.zeros((64, 128), F32)
            for m in range(4):
                x, g = slice(128 * m, 128 * m + 128), slice(512 + 64 * m, 576 + 64 * m)
                total += dot(full[at, g], parts[at, x], 0, 0)
                total += dot(parts[at, g], full[at, x], 0, 0)
            out[:, 2 * e : 2 * e + 2] = total.reshape(32, 2, 128)

    mover = lax.rem(lax.axis_index("par"), 2) == CHAIN

    @pl.when(mover)
    def _():
        add_up(keep, got)

    @pl.when(jnp.logical_not(mover))
    def _():
        add_up(got, keep)


def move_rows(part, ranks, up_right, down_left, inputs, other):
    pieces = lax.all_to_all(part, "par", 0, 0, tiled=True, axis_index_groups=CHIPS)
    total = jnp.sum(pieces.astype(F32), axis=0).astype(BF)
    full = spread(total, "par", CHIPS).reshape(2, 256, 768)
    return full[0], full[1]


def gather_ranks(part, ranks, up_right, down_left, inputs, other):
    along_z = spread(ranks, "ex", Z_HI).reshape(512, 128)
    gathered = spread(along_z, "ex", Y).reshape(16, 128, 128)
    return parts(gathered, up_right, down_left, inputs, other)


def per_device(*args):
    inputs, (lora_a, lora_b, up_left, up_right, down_left, down_right) = args[:6], args[6:]

    down_left = down_left.transpose(0, 2, 1).reshape(2, 128, 128)
    own = pack(inputs, down_right, up_left, lora_a, lora_b)
    other = lax.ppermute(own, "par", PAIR)
    part, ranks, far = first(own, other)
    mover = lax.axis_index("par") % 2 == CHAIN
    rows = [a.reshape(512, 128) for a in inputs]
    operands = part, ranks, up_right, down_left, rows, far
    keep, send = lax.cond(mover, move_rows, gather_ranks, *operands)
    got = lax.ppermute(send, "par", PAIR)
    out = call(join_kernel, [((32, 4, 128), F32)], keep, got)[0]
    out = lax.all_to_all(out, "par", 0, 0, tiled=True)
    out = jnp.sum(out.reshape(16, 4, 2, 128), axis=0) * (1.0 / 128)
    return out.reshape(4, 256)


def solution(mesh):
    in_specs = (P("ex", None, "par"),) * 6 + (
        P(None, "ex", "par"),
        P(None, "par", "ex"),
        P(None, "par", None),
        P(),
        P(),
        P(None, "par", None),
    )
    return jax.shard_map(
        per_device, mesh=mesh, in_specs=in_specs, out_specs=P("ex", "par"), check_vma=False
    )
```

```python
import jax
import jax.numpy as jnp
from jax import lax
from jax.experimental import pallas as pl
from jax.experimental.pallas import tpu as pltpu
from jax.sharding import PartitionSpec as P

BF = jnp.bfloat16
F32 = jnp.float32

Z_HI = [[4 * y + z for z in range(4)] for y in range(4)]
Y = [[4 * y + z for y in range(4)] for z in range(4)]
CHIPS = [[2 * chip + core for chip in range(16)] for core in range(2)]
PAIR = [(i, i ^ 1) for i in range(32)]
CHAIN = 1
VMEM = pl.BlockSpec(memory_space=pltpu.VMEM)
HBM = pl.BlockSpec(memory_space=pl.ANY)
LOOSE = pl.BlockSpec(memory_space=pltpu.VMEM)


def call(kernel, outs, *operands, specs=None, scratch=(), place=pltpu.VMEM, out_specs=None):
    specs = specs or [VMEM] * len(operands)
    operands = [
        pltpu.with_memory_space_constraint(a, pltpu.VMEM) if spec is VMEM else a
        for a, spec in zip(operands, specs)
    ]
    return pl.pallas_call(
        kernel,
        out_shape=tuple(place(shape, dtype) for shape, dtype in outs),
        in_specs=specs,
        out_specs=out_specs or (VMEM,) * len(outs),
        scratch_shapes=scratch,
        name=kernel.__name__,
    )(*operands)


def dot(a, b, over_a, over_b):
    return lax.dot_general(a, b, (((over_a,), (over_b,)), ((), ())), preferred_element_type=F32)


def spread(block, axis, groups):
    count = len(groups[0])
    copies = jnp.broadcast_to(block[None], (count,) + block.shape)
    return lax.all_to_all(copies, axis, 0, 0, tiled=True, axis_index_groups=groups)


UL, DR, RANKS, ALL = 3072, 3328, 3840, 3904


def pack_kernel(*refs):
    inputs, (down_right, up_left, lora_a, lora_b, send, ranks, sem) = refs[:6], refs[6:]
    copies = [(lora_a, ranks.at[0]), (lora_b, ranks.at[1])]
    copies += [(inputs[k], send.at[pl.ds(512 * k, 512)]) for k in range(6)]
    copies.append((up_left, send.at[pl.ds(UL, 256)]))
    copies.append((down_right, send.at[pl.ds(DR, 512)]))
    copies = [pltpu.make_async_copy(a, b, sem) for a, b in copies]
    for copy in copies:
        copy.start()
    for copy in copies:
        copy.wait()
    a, b = ranks[0].astype(F32), ranks[1].astype(F32)
    parts = [v[8 * m : 8 * m + 8] for m in range(4) for v in (a, b)]
    send[RANKS:ALL] = jnp.concatenate(parts, axis=0).astype(BF)


def pack(inputs, down_right, up_left, lora_a, lora_b):
    return call(
        pack_kernel,
        [((ALL, 128), BF)],
        *[a.reshape(512, 128) for a in inputs],
        down_right.reshape(512, 128),
        up_left.transpose(0, 2, 1).reshape(256, 128),
        lora_a.reshape(32, 128),
        lora_b.transpose(0, 2, 1).reshape(32, 128),
        specs=[HBM] * 10,
        scratch=[pltpu.VMEM((2, 32, 128), BF), pltpu.SemaphoreType.DMA],
    )[0]


def rows_of(own, other, k):
    at = slice(512 * k, 512 * k + 512)
    return jnp.concatenate([own[at], other[at]], axis=1)


def pick(rows, half, weight, over):
    low, high = [dot(rows(2 + 2 * half + i), weight, 1, over) for i in range(2)]
    return jnp.where(lax.broadcasted_iota(jnp.int32, low.shape, 1) < 64, low, high)


def first_kernel(own, other, part, ranks, far, sem):
    role = lax.rem(lax.axis_index("par") + CHAIN, 2)
    ranks[:64] = own[RANKS:ALL]
    ranks[64:] = other[RANKS:ALL]

    def put(at, value):
        part[:, :, at : at + value.shape[1]] = value.astype(BF).reshape(16, 32, value.shape[1])

    def right(m):
        at = slice(DR + 128 * m, DR + 128 * m + 128)
        return jnp.concatenate([own[at], other[at]], axis=0)

    @pl.when(role == 0)
    def _():
        hidden = rows_of(own, other, 0)
        put(0, dot(hidden, jnp.concatenate([right(0), right(1)], axis=1), 1, 0))
        put(256, dot(hidden, right(2), 1, 0))
        put(384, dot(rows_of(own, other, 1), right(3), 1, 0))
        left = jnp.concatenate([own[UL:DR], other[UL:DR]], axis=1)
        for half in range(2):
            weight = left[128 * half : 128 * half + 128]
            put(512 + 128 * half, pick(lambda k: rows_of(own, other, k), half, weight, 1))

    @pl.when(role == 1)
    def _():
        copy = pltpu.make_async_copy(other.at[pl.ds(0, UL)], far, sem)
        copy.start()
        copy.wait()


def first(own, other):
    shapes = [((16, 32, 768), BF), ((128, 128), BF), ((UL, 128), BF)]
    return call(
        first_kernel,
        shapes,
        own,
        other,
        scratch=[pltpu.SemaphoreType.DMA],
        place=jax.ShapeDtypeStruct,
        out_specs=(VMEM, VMEM, HBM),
    )


ORDER = (0, 1, 3, 2)


def parts_kernel(gathered, up_right, down_left, *refs):
    inputs, (far, keep, send, for_a, for_b) = refs[:6], refs[6:]
    for m in range(4):
        for_a[m] = up_right[m].astype(F32)
    for half in range(2):
        for_b[half] = down_left[half].astype(F32).T
    z_hi = jnp.bitwise_and(lax.axis_index("ex"), 3)
    owners = [4 * y + jnp.bitwise_xor(z_hi, k) for y in range(4) for k in ORDER]
    owners = [pl.ds(pl.multiple_of(8 * owner, 8), 8) for owner in owners]
    nothing = jnp.zeros((8, 128), F32)
    left_half = lax.broadcasted_iota(jnp.int32, (256, 128), 1) < 64
    side = [[], []]
    for m in range(4):
        rows_a = [part for at in owners for part in (for_a[m, at, :], nothing)]
        rows_b = [part for at in owners for part in (nothing, for_b[m // 2, at, :])]
        rows_b = jnp.concatenate(rows_b, axis=0)
        rows_b = jnp.where(left_half if m % 2 == 0 else ~left_half, rows_b, 0.0)
        factor = jnp.concatenate([jnp.concatenate(rows_a, axis=0), rows_b], axis=1).astype(BF)
        for core in range(2):
            at = slice(64 * core + 16 * m, 64 * core + 16 * m + 16)
            ranks = gathered[:, at, :].reshape(256, 128)
            side[core].append(dot(ranks, factor, 0, 0).astype(BF))

    def weight(at, *modules):
        halves = [jnp.concatenate([half[m][:, at] for m in modules], axis=1) for half in side]
        return jnp.concatenate(halves, axis=0)

    def put(at, value):
        send[:, at : at + value.shape[1]] = value[:256].astype(BF)
        keep[:, at : at + value.shape[1]] = value[256:].astype(BF)

    x_at, g_at = slice(0, 128), slice(128, 256)
    def rows(k):
        return jnp.concatenate([inputs[k][...], far[512 * k : 512 * k + 512]], axis=1)

    hidden = rows(0)
    put(0, dot(hidden, weight(x_at, 0, 1), 1, 0))
    put(256, dot(hidden, weight(x_at, 2), 1, 0))
    put(384, dot(rows(1), weight(x_at, 3), 1, 0))
    for half in range(2):
        pair = weight(g_at, 2 * half) + weight(g_at, 2 * half + 1)
        put(512 + 128 * half, pick(rows, half, pair, 0))


def parts(gathered, up_right, down_left, inputs, other):
    return call(
        parts_kernel,
        [((256, 768), BF)] * 2,
        gathered,
        up_right,
        down_left,
        *inputs,
        other,
        specs=[VMEM, LOOSE, LOOSE] + [VMEM] * 7,
        scratch=[pltpu.VMEM((4, 128, 128), F32), pltpu.VMEM((2, 128, 128), F32)],
        place=jax.ShapeDtypeStruct,
    )


def join_kernel(keep, got, out):
    def add_up(full, parts):
        for e in range(2):
            at = slice(128 * e, 128 * e + 128)
            total = jnp.zeros((64, 128), F32)
            for m in range(4):
                x, g = slice(128 * m, 128 * m + 128), slice(512 + 64 * m, 576 + 64 * m)
                total += dot(full[at, g], parts[at, x], 0, 0)
                total += dot(parts[at, g], full[at, x], 0, 0)
            out[:, 2 * e : 2 * e + 2] = total.reshape(32, 2, 128)

    mover = lax.rem(lax.axis_index("par"), 2) == CHAIN

    @pl.when(mover)
    def _():
        add_up(keep, got)

    @pl.when(jnp.logical_not(mover))
    def _():
        add_up(got, keep)


def move_rows(part, ranks, up_right, down_left, inputs, other):
    pieces = lax.all_to_all(part, "par", 0, 0, tiled=True, axis_index_groups=CHIPS)
    total = jnp.sum(pieces.astype(F32), axis=0).astype(BF)
    full = spread(total, "par", CHIPS).reshape(2, 256, 768)
    return full[0], full[1]


def swap(block, step):
    places = [(32 * e + p, 32 * (e ^ step) + p) for e in range(16) for p in range(1 - CHAIN, 32, 2)]
    return lax.ppermute(block, ("ex", "par"), places)


def gather_ranks(part, ranks, up_right, down_left, inputs, other):
    two = jnp.stack([ranks, swap(ranks, 1)])
    along_z = jnp.concatenate([two, swap(two, 3)]).reshape(512, 128)
    gathered = spread(along_z, "ex", Y).reshape(16, 128, 128)
    return parts(gathered, up_right, down_left, inputs, other)


def per_device(*args):
    inputs, (lora_a, lora_b, up_left, up_right, down_left, down_right) = args[:6], args[6:]

    down_left = down_left.transpose(0, 2, 1).reshape(2, 128, 128)
    own = pack(inputs, down_right, up_left, lora_a, lora_b)
    other = lax.ppermute(own, "par", PAIR)
    part, ranks, far = first(own, other)
    mover = lax.axis_index("par") % 2 == CHAIN
    rows = [a.reshape(512, 128) for a in inputs]
    operands = part, ranks, up_right, down_left, rows, far
    keep, send = lax.cond(mover, move_rows, gather_ranks, *operands)
    got = lax.ppermute(send, "par", PAIR)
    out = call(join_kernel, [((32, 4, 128), F32)], keep, got)[0]
    out = lax.all_to_all(out, "par", 0, 0, tiled=True)
    out = jnp.sum(out.reshape(16, 4, 2, 128), axis=0) * (1.0 / 128)
    out = jnp.concatenate([out[2:], out[:2]])
    return out.reshape(4, 256)


def solution(mesh):
    in_specs = (P("ex", None, "par"),) * 6 + (
        P(None, "ex", "par"),
        P(None, "par", "ex"),
        P(None, "par", None),
        P(),
        P(),
        P(None, "par", None),
    )
    return jax.shard_map(
        per_device, mesh=mesh, in_specs=in_specs, out_specs=P("ex", "par"), check_vma=False
    )
```

```python
import jax
import jax.numpy as jnp
from jax import lax
from jax.experimental import pallas as pl
from jax.experimental.pallas import tpu as pltpu
from jax.sharding import PartitionSpec as P

BF = jnp.bfloat16
F32 = jnp.float32

Z_HI = [[4 * y + z for z in range(4)] for y in range(4)]
Y = [[4 * y + z for y in range(4)] for z in range(4)]
CHIPS = [[2 * chip + core for chip in range(16)] for core in range(2)]
PAIR = [(i, i ^ 1) for i in range(32)]
CHAIN = 1
VMEM = pl.BlockSpec(memory_space=pltpu.VMEM)
HBM = pl.BlockSpec(memory_space=pl.ANY)
LOOSE = pl.BlockSpec(memory_space=pltpu.VMEM)


def call(kernel, outs, *operands, specs=None, scratch=(), place=pltpu.VMEM, out_specs=None):
    specs = specs or [VMEM] * len(operands)
    operands = [
        pltpu.with_memory_space_constraint(a, pltpu.VMEM) if spec is VMEM else a
        for a, spec in zip(operands, specs)
    ]
    return pl.pallas_call(
        kernel,
        out_shape=tuple(place(shape, dtype) for shape, dtype in outs),
        in_specs=specs,
        out_specs=out_specs or (VMEM,) * len(outs),
        scratch_shapes=scratch,
        name=kernel.__name__,
    )(*operands)


def dot(a, b, over_a, over_b):
    return lax.dot_general(a, b, (((over_a,), (over_b,)), ((), ())), preferred_element_type=F32)


def spread(block, axis, groups):
    count = len(groups[0])
    copies = jnp.broadcast_to(block[None], (count,) + block.shape)
    return lax.all_to_all(copies, axis, 0, 0, tiled=True, axis_index_groups=groups)


UL, DR, RANKS, ALL = 3072, 3328, 3840, 3904


def pack_kernel(*refs):
    inputs, (down_right, up_left, lora_a, lora_b, send, ranks, sem) = refs[:6], refs[6:]
    copies = [(lora_a, ranks.at[0]), (lora_b, ranks.at[1])]
    copies += [(inputs[k], send.at[pl.ds(512 * k, 512)]) for k in range(6)]
    copies.append((up_left, send.at[pl.ds(UL, 256)]))
    copies.append((down_right, send.at[pl.ds(DR, 512)]))
    copies = [pltpu.make_async_copy(a, b, sem) for a, b in copies]
    for copy in copies:
        copy.start()
    for copy in copies:
        copy.wait()
    a, b = ranks[0].astype(F32), ranks[1].astype(F32)
    parts = [v[8 * m : 8 * m + 8] for m in range(4) for v in (a, b)]
    send[RANKS:ALL] = jnp.concatenate(parts, axis=0).astype(BF)


def pack(inputs, down_right, up_left, lora_a, lora_b):
    return call(
        pack_kernel,
        [((ALL, 128), BF)],
        *[a.reshape(512, 128) for a in inputs],
        down_right.reshape(512, 128),
        up_left.transpose(0, 2, 1).reshape(256, 128),
        lora_a.reshape(32, 128),
        lora_b.transpose(0, 2, 1).reshape(32, 128),
        specs=[HBM] * 10,
        scratch=[pltpu.VMEM((2, 32, 128), BF), pltpu.SemaphoreType.DMA],
    )[0]


def rows_of(own, other, k):
    at = slice(512 * k, 512 * k + 512)
    return jnp.concatenate([own[at], other[at]], axis=1)


def pick(rows, half, weight, over):
    low, high = [dot(rows(2 + 2 * half + i), weight, 1, over) for i in range(2)]
    return jnp.where(lax.broadcasted_iota(jnp.int32, low.shape, 1) < 64, low, high)


def first_kernel(own, other, part, ranks, far, rows, sem):
    role = lax.rem(lax.axis_index("par") + CHAIN, 2)
    ranks[:64] = own[RANKS:ALL]
    ranks[64:] = other[RANKS:ALL]
    copies = []

    def put(at, value):
        columns = slice(at, at + value.shape[1])
        rows[:, :, columns] = value.astype(BF).reshape(16, 32, value.shape[1])
        copies.append(pltpu.make_async_copy(rows.at[:, :, columns], part.at[:, :, columns], sem))
        copies[-1].start()

    def right(m):
        at = slice(DR + 128 * m, DR + 128 * m + 128)
        return jnp.concatenate([own[at], other[at]], axis=0)

    @pl.when(role == 0)
    def _():
        left = jnp.concatenate([own[UL:DR], other[UL:DR]], axis=1)
        for half in range(2):
            weight = left[128 * half : 128 * half + 128]
            put(512 + 128 * half, pick(lambda k: rows_of(own, other, k), half, weight, 1))
        hidden = rows_of(own, other, 0)
        put(0, dot(hidden, jnp.concatenate([right(0), right(1)], axis=1), 1, 0))
        put(256, dot(hidden, right(2), 1, 0))
        put(384, dot(rows_of(own, other, 1), right(3), 1, 0))
        for copy in copies:
            copy.wait()

    @pl.when(role == 1)
    def _():
        copy = pltpu.make_async_copy(other.at[pl.ds(0, UL)], far, sem)
        copy.start()
        copy.wait()


def first(own, other):
    shapes = [((16, 32, 768), BF), ((128, 128), BF), ((UL, 128), BF)]
    return call(
        first_kernel,
        shapes,
        own,
        other,
        scratch=[pltpu.VMEM((16, 32, 768), BF), pltpu.SemaphoreType.DMA],
        place=jax.ShapeDtypeStruct,
        out_specs=(HBM, VMEM, HBM),
    )


ORDER = (0, 1, 3, 2)


def parts_kernel(gathered, up_right, down_left, *refs):
    inputs, (far, keep, send, for_a, for_b) = refs[:6], refs[6:]
    for m in range(4):
        for_a[m] = up_right[m].astype(F32)
    for half in range(2):
        for_b[half] = down_left[half].astype(F32).T
    z_hi = jnp.bitwise_and(lax.axis_index("ex"), 3)
    owners = [4 * y + jnp.bitwise_xor(z_hi, k) for y in range(4) for k in ORDER]
    owners = [pl.ds(pl.multiple_of(8 * owner, 8), 8) for owner in owners]
    nothing = jnp.zeros((8, 128), F32)
    left_half = lax.broadcasted_iota(jnp.int32, (256, 128), 1) < 64
    side = [[], []]
    for m in range(4):
        rows_a = [part for at in owners for part in (for_a[m, at, :], nothing)]
        rows_b = [part for at in owners for part in (nothing, for_b[m // 2, at, :])]
        rows_b = jnp.concatenate(rows_b, axis=0)
        rows_b = jnp.where(left_half if m % 2 == 0 else ~left_half, rows_b, 0.0)
        factor = jnp.concatenate([jnp.concatenate(rows_a, axis=0), rows_b], axis=1).astype(BF)
        for core in range(2):
            at = slice(64 * core + 16 * m, 64 * core + 16 * m + 16)
            ranks = gathered[:, at, :].reshape(256, 128)
            side[core].append(dot(ranks, factor, 0, 0).astype(BF))

    def weight(at, *modules):
        halves = [jnp.concatenate([half[m][:, at] for m in modules], axis=1) for half in side]
        return jnp.concatenate(halves, axis=0)

    def put(at, value):
        send[:, at : at + value.shape[1]] = value[:256].astype(BF)
        keep[:, at : at + value.shape[1]] = value[256:].astype(BF)

    x_at, g_at = slice(0, 128), slice(128, 256)
    def rows(k):
        return jnp.concatenate([inputs[k][...], far[512 * k : 512 * k + 512]], axis=1)

    hidden = rows(0)
    put(0, dot(hidden, weight(x_at, 0, 1), 1, 0))
    put(256, dot(hidden, weight(x_at, 2), 1, 0))
    put(384, dot(rows(1), weight(x_at, 3), 1, 0))
    for half in range(2):
        pair = weight(g_at, 2 * half) + weight(g_at, 2 * half + 1)
        put(512 + 128 * half, pick(rows, half, pair, 0))


def parts(gathered, up_right, down_left, inputs, other):
    return call(
        parts_kernel,
        [((256, 768), BF)] * 2,
        gathered,
        up_right,
        down_left,
        *inputs,
        other,
        specs=[VMEM, LOOSE, LOOSE] + [VMEM] * 7,
        scratch=[pltpu.VMEM((4, 128, 128), F32), pltpu.VMEM((2, 128, 128), F32)],
        place=jax.ShapeDtypeStruct,
    )


def join_kernel(keep, got, out):
    def add_up(full, parts):
        for e in range(2):
            at = slice(128 * e, 128 * e + 128)
            total = jnp.zeros((64, 128), F32)
            for m in range(4):
                x, g = slice(128 * m, 128 * m + 128), slice(512 + 64 * m, 576 + 64 * m)
                total += dot(full[at, g], parts[at, x], 0, 0)
                total += dot(parts[at, g], full[at, x], 0, 0)
            out[:, 2 * e : 2 * e + 2] = total.reshape(32, 2, 128)

    mover = lax.rem(lax.axis_index("par"), 2) == CHAIN

    @pl.when(mover)
    def _():
        add_up(keep, got)

    @pl.when(jnp.logical_not(mover))
    def _():
        add_up(got, keep)


def move_rows(part, ranks, up_right, down_left, inputs, other):
    pieces = lax.all_to_all(part, "par", 0, 0, tiled=True, axis_index_groups=CHIPS)
    total = jnp.sum(pieces.astype(F32), axis=0).astype(BF)
    full = spread(total, "par", CHIPS).reshape(2, 256, 768)
    return full[0], full[1]


def swap(block, step):
    places = [(32 * e + p, 32 * (e ^ step) + p) for e in range(16) for p in range(1 - CHAIN, 32, 2)]
    return lax.ppermute(block, ("ex", "par"), places)


def gather_ranks(part, ranks, up_right, down_left, inputs, other):
    two = jnp.stack([ranks, swap(ranks, 1)])
    along_z = jnp.concatenate([two, swap(two, 3)]).reshape(512, 128)
    gathered = spread(along_z, "ex", Y).reshape(16, 128, 128)
    return parts(gathered, up_right, down_left, inputs, other)


def per_device(*args):
    inputs, (lora_a, lora_b, up_left, up_right, down_left, down_right) = args[:6], args[6:]

    down_left = down_left.transpose(0, 2, 1).reshape(2, 128, 128)
    own = pack(inputs, down_right, up_left, lora_a, lora_b)
    other = lax.ppermute(own, "par", PAIR)
    part, ranks, far = first(own, other)
    mover = lax.axis_index("par") % 2 == CHAIN
    rows = [a.reshape(512, 128) for a in inputs]
    operands = part, ranks, up_right, down_left, rows, far
    keep, send = lax.cond(mover, move_rows, gather_ranks, *operands)
    got = lax.ppermute(send, "par", PAIR)
    out = call(join_kernel, [((32, 4, 128), F32)], keep, got)[0]
    out = lax.all_to_all(out, "par", 0, 0, tiled=True)
    out = jnp.sum(out.reshape(16, 4, 2, 128), axis=0) * (1.0 / 128)
    out = jnp.concatenate([out[2:], out[:2]])
    return out.reshape(4, 256)


def solution(mesh):
    in_specs = (P("ex", None, "par"),) * 6 + (
        P(None, "ex", "par"),
        P(None, "par", "ex"),
        P(None, "par", None),
        P(),
        P(),
        P(None, "par", None),
    )
    return jax.shard_map(
        per_device, mesh=mesh, in_specs=in_specs, out_specs=P("ex", "par"), check_vma=False
    )
```

```python
import jax
import jax.numpy as jnp
from jax import lax
from jax.experimental import pallas as pl
from jax.experimental.pallas import tpu as pltpu
from jax.sharding import PartitionSpec as P

BF = jnp.bfloat16
F32 = jnp.float32

Z_HI = [[4 * y + z for z in range(4)] for y in range(4)]
Y = [[4 * y + z for y in range(4)] for z in range(4)]
CHIPS = [[2 * chip + core for chip in range(16)] for core in range(2)]
PAIR = [(i, i ^ 1) for i in range(32)]
CHAIN = 1
VMEM = pl.BlockSpec(memory_space=pltpu.VMEM)
HBM = pl.BlockSpec(memory_space=pl.ANY)
LOOSE = pl.BlockSpec(memory_space=pltpu.VMEM)


def call(kernel, outs, *operands, specs=None, scratch=(), place=pltpu.VMEM, out_specs=None):
    specs = specs or [VMEM] * len(operands)
    operands = [
        pltpu.with_memory_space_constraint(a, pltpu.VMEM) if spec is VMEM else a
        for a, spec in zip(operands, specs)
    ]
    return pl.pallas_call(
        kernel,
        out_shape=tuple(place(shape, dtype) for shape, dtype in outs),
        in_specs=specs,
        out_specs=out_specs or (VMEM,) * len(outs),
        scratch_shapes=scratch,
        name=kernel.__name__,
    )(*operands)


def dot(a, b, over_a, over_b):
    return lax.dot_general(a, b, (((over_a,), (over_b,)), ((), ())), preferred_element_type=F32)


def spread(block, axis, groups):
    count = len(groups[0])
    copies = jnp.broadcast_to(block[None], (count,) + block.shape)
    return lax.all_to_all(copies, axis, 0, 0, tiled=True, axis_index_groups=groups)


UL, DR, RANKS, ALL = 3072, 3328, 3840, 3904


def pack_kernel(*refs):
    inputs, (down_right, up_left, lora_a, lora_b, send, ranks, sem) = refs[:6], refs[6:]
    copies = [(lora_a, ranks.at[0]), (lora_b, ranks.at[1])]
    copies += [(inputs[k], send.at[pl.ds(512 * k, 512)]) for k in range(6)]
    copies.append((up_left, send.at[pl.ds(UL, 256)]))
    copies.append((down_right, send.at[pl.ds(DR, 512)]))
    copies = [pltpu.make_async_copy(a, b, sem) for a, b in copies]
    for copy in copies:
        copy.start()
    for copy in copies:
        copy.wait()
    a, b = ranks[0].astype(F32), ranks[1].astype(F32)
    parts = [v[8 * m : 8 * m + 8] for m in range(4) for v in (a, b)]
    send[RANKS:ALL] = jnp.concatenate(parts, axis=0).astype(BF)


def pack(inputs, down_right, up_left, lora_a, lora_b):
    return call(
        pack_kernel,
        [((ALL, 128), BF)],
        *[a.reshape(512, 128) for a in inputs],
        down_right.reshape(512, 128),
        up_left.transpose(0, 2, 1).reshape(256, 128),
        lora_a.reshape(32, 128),
        lora_b.transpose(0, 2, 1).reshape(32, 128),
        specs=[HBM] * 10,
        scratch=[pltpu.VMEM((2, 32, 128), BF), pltpu.SemaphoreType.DMA],
    )[0]


def rows_of(own, other, k):
    at = slice(512 * k, 512 * k + 512)
    return jnp.concatenate([own[at], other[at]], axis=1)


def pick(rows, half, weight, over):
    low, high = [dot(rows(2 + 2 * half + i), weight, 1, over) for i in range(2)]
    return jnp.where(lax.broadcasted_iota(jnp.int32, low.shape, 1) < 64, low, high)


def first_kernel(own, other, part, ranks, far, rows, sem):
    role = lax.rem(lax.axis_index("par") + CHAIN, 2)
    ranks[:64] = own[RANKS:ALL]
    ranks[64:] = other[RANKS:ALL]
    copies = []

    def put(at, value):
        columns = slice(at, at + value.shape[1])
        rows[:, :, columns] = value.astype(BF).reshape(16, 32, value.shape[1])
        copies.append(pltpu.make_async_copy(rows.at[:, :, columns], part.at[:, :, columns], sem))
        copies[-1].start()

    def right(m):
        at = slice(DR + 128 * m, DR + 128 * m + 128)
        return jnp.concatenate([own[at], other[at]], axis=0)

    @pl.when(role == 0)
    def _():
        left = jnp.concatenate([own[UL:DR], other[UL:DR]], axis=1)
        for half in range(2):
            weight = left[128 * half : 128 * half + 128]
            put(512 + 128 * half, pick(lambda k: rows_of(own, other, k), half, weight, 1))
        hidden = rows_of(own, other, 0)
        put(0, dot(hidden, jnp.concatenate([right(0), right(1)], axis=1), 1, 0))
        put(256, dot(hidden, right(2), 1, 0))
        put(384, dot(rows_of(own, other, 1), right(3), 1, 0))
        for copy in copies:
            copy.wait()

    @pl.when(role == 1)
    def _():
        copy = pltpu.make_async_copy(other.at[pl.ds(0, UL)], far, sem)
        copy.start()
        copy.wait()


def first(own, other):
    shapes = [((16, 32, 768), BF), ((128, 128), BF), ((UL, 128), BF)]
    return call(
        first_kernel,
        shapes,
        own,
        other,
        scratch=[pltpu.VMEM((16, 32, 768), BF), pltpu.SemaphoreType.DMA],
        place=jax.ShapeDtypeStruct,
        out_specs=(HBM, VMEM, HBM),
    )


ORDER = (0, 1, 3, 2)


def parts_kernel(gathered, up_right, down_left, *refs):
    inputs, (far, keep, send, for_a, for_b) = refs[:6], refs[6:]
    for m in range(4):
        for_a[m] = up_right[m].astype(F32)
    for half in range(2):
        for_b[half] = down_left[half].astype(F32).T
    z_hi = jnp.bitwise_and(lax.axis_index("ex"), 3)
    owners = [4 * y + jnp.bitwise_xor(z_hi, k) for y in range(4) for k in ORDER]
    owners = [pl.ds(pl.multiple_of(8 * owner, 8), 8) for owner in owners]
    nothing = jnp.zeros((8, 128), F32)
    left_half = lax.broadcasted_iota(jnp.int32, (256, 128), 1) < 64
    side = [[], []]
    for m in range(4):
        rows_a = [part for at in owners for part in (for_a[m, at, :], nothing)]
        rows_b = [part for at in owners for part in (nothing, for_b[m // 2, at, :])]
        rows_b = jnp.concatenate(rows_b, axis=0)
        rows_b = jnp.where(left_half if m % 2 == 0 else ~left_half, rows_b, 0.0)
        factor = jnp.concatenate([jnp.concatenate(rows_a, axis=0), rows_b], axis=1).astype(BF)
        for core in range(2):
            at = slice(64 * core + 16 * m, 64 * core + 16 * m + 16)
            ranks = gathered[:, at, :].reshape(256, 128)
            side[core].append(dot(ranks, factor, 0, 0).astype(BF))

    def weight(at, *modules):
        halves = [jnp.concatenate([half[m][:, at] for m in modules], axis=1) for half in side]
        return jnp.concatenate(halves, axis=0)

    def put(at, value):
        send[:, at : at + value.shape[1]] = value[:256].astype(BF)
        keep[:, at : at + value.shape[1]] = value[256:].astype(BF)

    x_at, g_at = slice(0, 128), slice(128, 256)
    def rows(k):
        return jnp.concatenate([inputs[k][...], far[512 * k : 512 * k + 512]], axis=1)

    hidden = rows(0)
    put(0, dot(hidden, weight(x_at, 0, 1), 1, 0))
    put(256, dot(hidden, weight(x_at, 2), 1, 0))
    put(384, dot(rows(1), weight(x_at, 3), 1, 0))
    for half in range(2):
        pair = weight(g_at, 2 * half) + weight(g_at, 2 * half + 1)
        put(512 + 128 * half, pick(rows, half, pair, 0))


def parts(gathered, up_right, down_left, inputs, other):
    return call(
        parts_kernel,
        [((256, 768), BF)] * 2,
        gathered,
        up_right,
        down_left,
        *inputs,
        other,
        specs=[VMEM, LOOSE, LOOSE] + [VMEM] * 7,
        scratch=[pltpu.VMEM((4, 128, 128), F32), pltpu.VMEM((2, 128, 128), F32)],
        place=jax.ShapeDtypeStruct,
    )


def join_kernel(keep, got, out):
    def add_up(full, parts):
        for e in range(2):
            at = slice(128 * e, 128 * e + 128)
            total = jnp.zeros((64, 128), F32)
            for m in range(4):
                x, g = slice(128 * m, 128 * m + 128), slice(512 + 64 * m, 576 + 64 * m)
                total += dot(full[at, g], parts[at, x], 0, 0)
                total += dot(parts[at, g], full[at, x], 0, 0)
            out[:, 2 * e : 2 * e + 2] = total.reshape(32, 2, 128)

    mover = lax.rem(lax.axis_index("par"), 2) == CHAIN

    @pl.when(mover)
    def _():
        add_up(keep, got)

    @pl.when(jnp.logical_not(mover))
    def _():
        add_up(got, keep)


def move_rows(part, ranks, up_right, down_left, inputs, other):
    pieces = lax.all_to_all(part, "par", 0, 0, tiled=True, axis_index_groups=CHIPS)
    total = jnp.sum(pieces.astype(F32), axis=0).astype(BF)
    full = spread(total, "par", CHIPS).reshape(2, 256, 768)
    return full[0], full[1]


def swap(block, step):
    places = [(32 * e + p, 32 * (e ^ step) + p) for e in range(16) for p in range(1 - CHAIN, 32, 2)]
    return lax.ppermute(block, ("ex", "par"), places)


def gather_ranks(part, ranks, up_right, down_left, inputs, other):
    two = jnp.stack([ranks, swap(ranks, 1)])
    along_z = jnp.concatenate([two, swap(two, 3)]).reshape(512, 128)
    gathered = spread(along_z, "ex", Y).reshape(16, 128, 128)
    return parts(gathered, up_right, down_left, inputs, other)


def place_kernel(pieces, out):
    total = [pieces[core] for core in range(2)]
    for chip in range(1, 16):
        total = [total[core] + pieces[2 * chip + core] for core in range(2)]
    for e in range(4):
        rows = total[CHAIN if e < 2 else 1 - CHAIN] * (1.0 / 128)
        for i in range(2):
            at = 2 * (e % 2) + i
            out[e : e + 1, 128 * i : 128 * i + 128] = rows[at : at + 1]


def per_device(*args):
    inputs, (lora_a, lora_b, up_left, up_right, down_left, down_right) = args[:6], args[6:]

    down_left = down_left.transpose(0, 2, 1).reshape(2, 128, 128)
    own = pack(inputs, down_right, up_left, lora_a, lora_b)
    other = lax.ppermute(own, "par", PAIR)
    part, ranks, far = first(own, other)
    mover = lax.axis_index("par") % 2 == CHAIN
    rows = [a.reshape(512, 128) for a in inputs]
    operands = part, ranks, up_right, down_left, rows, far
    keep, send = lax.cond(mover, move_rows, gather_ranks, *operands)
    got = lax.ppermute(send, "par", PAIR)
    out = call(join_kernel, [((32, 4, 128), F32)], keep, got)[0]
    out = lax.all_to_all(out, "par", 0, 0, tiled=True)
    return call(place_kernel, [((4, 256), F32)], out, place=jax.ShapeDtypeStruct)[0]


def solution(mesh):
    in_specs = (P("ex", None, "par"),) * 6 + (
        P(None, "ex", "par"),
        P(None, "par", "ex"),
        P(None, "par", None),
        P(),
        P(),
        P(None, "par", None),
    )
    return jax.shard_map(
        per_device, mesh=mesh, in_specs=in_specs, out_specs=P("ex", "par"), check_vma=False
    )
```

```python
import jax
import jax.numpy as jnp
from jax import lax
from jax.experimental import pallas as pl
from jax.experimental.pallas import tpu as pltpu
from jax.sharding import PartitionSpec as P

BF = jnp.bfloat16
F32 = jnp.float32

Z_HI = [[4 * y + z for z in range(4)] for y in range(4)]
Y = [[4 * y + z for y in range(4)] for z in range(4)]
CHIPS = [[2 * chip + core for chip in range(16)] for core in range(2)]
PAIR = [(i, i ^ 1) for i in range(32)]
CHAIN = 1
VMEM = pl.BlockSpec(memory_space=pltpu.VMEM)
HBM = pl.BlockSpec(memory_space=pl.ANY)
LOOSE = pl.BlockSpec(memory_space=pltpu.VMEM)


def call(kernel, outs, *operands, specs=None, scratch=(), place=pltpu.VMEM, out_specs=None):
    specs = specs or [VMEM] * len(operands)
    operands = [
        pltpu.with_memory_space_constraint(a, pltpu.VMEM) if spec is VMEM else a
        for a, spec in zip(operands, specs)
    ]
    return pl.pallas_call(
        kernel,
        out_shape=tuple(place(shape, dtype) for shape, dtype in outs),
        in_specs=specs,
        out_specs=out_specs or (VMEM,) * len(outs),
        scratch_shapes=scratch,
        name=kernel.__name__,
    )(*operands)


def dot(a, b, over_a, over_b):
    return lax.dot_general(a, b, (((over_a,), (over_b,)), ((), ())), preferred_element_type=F32)


def spread(block, axis, groups):
    count = len(groups[0])
    copies = jnp.broadcast_to(block[None], (count,) + block.shape)
    return lax.all_to_all(copies, axis, 0, 0, tiled=True, axis_index_groups=groups)


UL, DR, RANKS, ALL = 3072, 3328, 3840, 3904


def pack_kernel(*refs):
    inputs, (down_right, up_left, lora_a, lora_b, send, ranks, sem) = refs[:6], refs[6:]
    copies = [(lora_a, ranks.at[0]), (lora_b, ranks.at[1])]
    copies += [(inputs[k], send.at[pl.ds(512 * k, 512)]) for k in range(6)]
    copies.append((up_left, send.at[pl.ds(UL, 256)]))
    copies.append((down_right, send.at[pl.ds(DR, 512)]))
    copies = [pltpu.make_async_copy(a, b, sem) for a, b in copies]
    for copy in copies:
        copy.start()
    for copy in copies:
        copy.wait()
    a, b = ranks[0].astype(F32), ranks[1].astype(F32)
    parts = [v[8 * m : 8 * m + 8] for m in range(4) for v in (a, b)]
    send[RANKS:ALL] = jnp.concatenate(parts, axis=0).astype(BF)


def pack(inputs, down_right, up_left, lora_a, lora_b):
    return call(
        pack_kernel,
        [((ALL, 128), BF)],
        *[a.reshape(512, 128) for a in inputs],
        down_right.reshape(512, 128),
        up_left.transpose(0, 2, 1).reshape(256, 128),
        lora_a.reshape(32, 128),
        lora_b.transpose(0, 2, 1).reshape(32, 128),
        specs=[HBM] * 10,
        scratch=[pltpu.VMEM((2, 32, 128), BF), pltpu.SemaphoreType.DMA],
    )[0]


def rows_of(own, other, k):
    at = slice(512 * k, 512 * k + 512)
    return jnp.concatenate([own[at], other[at]], axis=1)


def first_kernel(own, other, part, ranks, far, rows, sem):
    role = lax.rem(lax.axis_index("par") + CHAIN, 2)
    ranks[:64] = own[RANKS:ALL]
    ranks[64:] = other[RANKS:ALL]
    copies = []

    def put(at, value):
        columns = slice(at, at + value.shape[1])
        rows[:, :, columns] = value.astype(BF).reshape(16, 32, value.shape[1])
        copies.append(pltpu.make_async_copy(rows.at[:, :, columns], part.at[:, :, columns], sem))
        copies[-1].start()

    def right(m):
        at = slice(DR + 128 * m, DR + 128 * m + 128)
        return jnp.concatenate([own[at], other[at]], axis=0)

    @pl.when(role == 0)
    def _():
        left = jnp.concatenate([own[UL:DR], other[UL:DR]], axis=1)
        for half in range(2):
            weight = left[128 * half : 128 * half + 128]
            low = lax.broadcasted_iota(jnp.int32, weight.shape, 0) < 64
            zero = jnp.zeros_like(weight)
            weight = [jnp.where(low, weight, zero), jnp.where(low, zero, weight)]
            grads = [rows_of(own, other, 2 + 2 * half + i) for i in range(2)]
            weight, grads = (jnp.concatenate(v, axis=1) for v in (weight, grads))
            put(512 + 128 * half, dot(grads, weight, 1, 1))
        hidden = rows_of(own, other, 0)
        put(0, dot(hidden, jnp.concatenate([right(0), right(1)], axis=1), 1, 0))
        put(256, dot(hidden, right(2), 1, 0))
        put(384, dot(rows_of(own, other, 1), right(3), 1, 0))
        for copy in copies:
            copy.wait()

    @pl.when(role == 1)
    def _():
        copy = pltpu.make_async_copy(other.at[pl.ds(0, UL)], far, sem)
        copy.start()
        copy.wait()


def first(own, other):
    shapes = [((16, 32, 768), BF), ((128, 128), BF), ((UL, 128), BF)]
    return call(
        first_kernel,
        shapes,
        own,
        other,
        scratch=[pltpu.VMEM((16, 32, 768), BF), pltpu.SemaphoreType.DMA],
        place=jax.ShapeDtypeStruct,
        out_specs=(HBM, VMEM, HBM),
    )


ORDER = (0, 1, 3, 2)


def parts_kernel(gathered, up_right, down_left, *refs):
    inputs, (far, keep, send, for_a, for_b) = refs[:6], refs[6:]
    for m in range(4):
        for_a[m] = up_right[m].astype(F32)
    for half in range(2):
        for_b[half] = down_left[half].astype(F32).T
    z_hi = jnp.bitwise_and(lax.axis_index("ex"), 3)
    owners = [4 * y + jnp.bitwise_xor(z_hi, k) for y in range(4) for k in ORDER]
    owners = [pl.ds(pl.multiple_of(8 * owner, 8), 8) for owner in owners]
    nothing = jnp.zeros((8, 128), F32)
    left_half = lax.broadcasted_iota(jnp.int32, (256, 128), 1) < 64
    side = [[], []]
    for m in range(4):
        rows_a = [part for at in owners for part in (for_a[m, at, :], nothing)]
        rows_b = [part for at in owners for part in (nothing, for_b[m // 2, at, :])]
        rows_b = jnp.concatenate(rows_b, axis=0)
        rows_b = jnp.where(left_half if m % 2 == 0 else ~left_half, rows_b, 0.0)
        factor = jnp.concatenate([jnp.concatenate(rows_a, axis=0), rows_b], axis=1).astype(BF)
        for core in range(2):
            at = slice(64 * core + 16 * m, 64 * core + 16 * m + 16)
            ranks = gathered[:, at, :].reshape(256, 128)
            side[core].append(dot(ranks, factor, 0, 0).astype(BF))

    def weight(at, *modules):
        halves = [jnp.concatenate([half[m][:, at] for m in modules], axis=1) for half in side]
        return jnp.concatenate(halves, axis=0)

    def put(at, value):
        send[:, at : at + value.shape[1]] = value[:256].astype(BF)
        keep[:, at : at + value.shape[1]] = value[256:].astype(BF)

    x_at, g_at = slice(0, 128), slice(128, 256)
    def rows(k):
        return jnp.concatenate([inputs[k][...], far[512 * k : 512 * k + 512]], axis=1)

    hidden = rows(0)
    put(0, dot(hidden, weight(x_at, 0, 1), 1, 0))
    put(256, dot(hidden, weight(x_at, 2), 1, 0))
    put(384, dot(rows(1), weight(x_at, 3), 1, 0))
    for half in range(2):
        pair = jnp.concatenate([weight(g_at, 2 * half + i) for i in range(2)], axis=0)
        grads = jnp.concatenate([rows(2 + 2 * half + i) for i in range(2)], axis=1)
        put(512 + 128 * half, dot(grads, pair, 1, 0))


def parts(gathered, up_right, down_left, inputs, other):
    return call(
        parts_kernel,
        [((256, 768), BF)] * 2,
        gathered,
        up_right,
        down_left,
        *inputs,
        other,
        specs=[VMEM, LOOSE, LOOSE] + [VMEM] * 7,
        scratch=[pltpu.VMEM((4, 128, 128), F32), pltpu.VMEM((2, 128, 128), F32)],
        place=jax.ShapeDtypeStruct,
    )


def join_kernel(keep, got, out):
    def add_up(full, parts):
        for e in range(2):
            at = slice(128 * e, 128 * e + 128)
            total = jnp.zeros((64, 128), F32)
            for m in range(4):
                x, g = slice(128 * m, 128 * m + 128), slice(512 + 64 * m, 576 + 64 * m)
                total += dot(full[at, g], parts[at, x], 0, 0)
                total += dot(parts[at, g], full[at, x], 0, 0)
            out[:, 2 * e : 2 * e + 2] = total.reshape(32, 2, 128)

    mover = lax.rem(lax.axis_index("par"), 2) == CHAIN

    @pl.when(mover)
    def _():
        add_up(keep, got)

    @pl.when(jnp.logical_not(mover))
    def _():
        add_up(got, keep)


def move_rows(part, ranks, up_right, down_left, inputs, other):
    pieces = lax.all_to_all(part, "par", 0, 0, tiled=True, axis_index_groups=CHIPS)
    total = jnp.sum(pieces.astype(F32), axis=0).astype(BF)
    full = spread(total, "par", CHIPS).reshape(2, 256, 768)
    return full[0], full[1]


def swap(block, step):
    places = [(32 * e + p, 32 * (e ^ step) + p) for e in range(16) for p in range(1 - CHAIN, 32, 2)]
    return lax.ppermute(block, ("ex", "par"), places)


def gather_ranks(part, ranks, up_right, down_left, inputs, other):
    two = jnp.stack([ranks, swap(ranks, 1)])
    along_z = jnp.concatenate([two, swap(two, 3)]).reshape(512, 128)
    gathered = spread(along_z, "ex", Y).reshape(16, 128, 128)
    return parts(gathered, up_right, down_left, inputs, other)


def place_kernel(pieces, out):
    total = [pieces[core] for core in range(2)]
    for chip in range(1, 16):
        total = [total[core] + pieces[2 * chip + core] for core in range(2)]
    for e in range(4):
        rows = total[CHAIN if e < 2 else 1 - CHAIN] * (1.0 / 128)
        for i in range(2):
            at = 2 * (e % 2) + i
            out[e : e + 1, 128 * i : 128 * i + 128] = rows[at : at + 1]


def per_device(*args):
    inputs, (lora_a, lora_b, up_left, up_right, down_left, down_right) = args[:6], args[6:]

    down_left = down_left.transpose(0, 2, 1).reshape(2, 128, 128)
    own = pack(inputs, down_right, up_left, lora_a, lora_b)
    other = lax.ppermute(own, "par", PAIR)
    part, ranks, far = first(own, other)
    mover = lax.axis_index("par") % 2 == CHAIN
    rows = [a.reshape(512, 128) for a in inputs]
    operands = part, ranks, up_right, down_left, rows, far
    keep, send = lax.cond(mover, move_rows, gather_ranks, *operands)
    got = lax.ppermute(send, "par", PAIR)
    out = call(join_kernel, [((32, 4, 128), F32)], keep, got)[0]
    out = lax.all_to_all(out, "par", 0, 0, tiled=True)
    return call(place_kernel, [((4, 256), F32)], out, place=jax.ShapeDtypeStruct)[0]


def solution(mesh):
    in_specs = (P("ex", None, "par"),) * 6 + (
        P(None, "ex", "par"),
        P(None, "par", "ex"),
        P(None, "par", None),
        P(),
        P(),
        P(None, "par", None),
    )
    return jax.shard_map(
        per_device, mesh=mesh, in_specs=in_specs, out_specs=P("ex", "par"), check_vma=False
    )
```

```python
import jax
import jax.numpy as jnp
from jax import lax
from jax.experimental import pallas as pl
from jax.experimental.pallas import tpu as pltpu
from jax.sharding import PartitionSpec as P

BF = jnp.bfloat16
F32 = jnp.float32

Z_HI = [[4 * y + z for z in range(4)] for y in range(4)]
Y = [[4 * y + z for y in range(4)] for z in range(4)]
CHIPS = [[2 * chip + core for chip in range(16)] for core in range(2)]
PAIR = [(i, i ^ 1) for i in range(32)]
CHAIN = 1
VMEM = pl.BlockSpec(memory_space=pltpu.VMEM)
HBM = pl.BlockSpec(memory_space=pl.ANY)
LOOSE = pl.BlockSpec(memory_space=pltpu.VMEM)


def call(kernel, outs, *operands, specs=None, scratch=(), place=pltpu.VMEM, out_specs=None):
    specs = specs or [VMEM] * len(operands)
    operands = [
        pltpu.with_memory_space_constraint(a, pltpu.VMEM) if spec is VMEM else a
        for a, spec in zip(operands, specs)
    ]
    return pl.pallas_call(
        kernel,
        out_shape=tuple(place(shape, dtype) for shape, dtype in outs),
        in_specs=specs,
        out_specs=out_specs or (VMEM,) * len(outs),
        scratch_shapes=scratch,
        name=kernel.__name__,
    )(*operands)


def dot(a, b, over_a, over_b):
    return lax.dot_general(a, b, (((over_a,), (over_b,)), ((), ())), preferred_element_type=F32)


def spread(block, axis, groups):
    count = len(groups[0])
    copies = jnp.broadcast_to(block[None], (count,) + block.shape)
    return lax.all_to_all(copies, axis, 0, 0, tiled=True, axis_index_groups=groups)


UL, DR, RANKS, ALL = 3072, 3328, 3840, 3904


def pack_kernel(*refs):
    inputs, (down_right, up_left, lora_a, lora_b, send, ranks, sem) = refs[:6], refs[6:]
    copies = [(lora_a, ranks.at[0]), (lora_b, ranks.at[1])]
    copies += [(inputs[k], send.at[pl.ds(512 * k, 512)]) for k in range(6)]
    copies.append((up_left, send.at[pl.ds(UL, 256)]))
    copies.append((down_right, send.at[pl.ds(DR, 512)]))
    copies = [pltpu.make_async_copy(a, b, sem) for a, b in copies]
    for copy in copies:
        copy.start()
    for copy in copies:
        copy.wait()
    a, b = ranks[0].astype(F32), ranks[1].astype(F32)
    parts = [v[8 * m : 8 * m + 8] for m in range(4) for v in (a, b)]
    send[RANKS:ALL] = jnp.concatenate(parts, axis=0).astype(BF)


def pack(inputs, down_right, up_left, lora_a, lora_b):
    return call(
        pack_kernel,
        [((ALL, 128), BF)],
        *[a.reshape(512, 128) for a in inputs],
        down_right.reshape(512, 128),
        up_left.transpose(0, 2, 1).reshape(256, 128),
        lora_a.reshape(32, 128),
        lora_b.transpose(0, 2, 1).reshape(32, 128),
        specs=[HBM] * 10,
        scratch=[pltpu.VMEM((2, 32, 128), BF), pltpu.SemaphoreType.DMA],
    )[0]


def rows_of(own, other, k):
    at = slice(512 * k, 512 * k + 512)
    return jnp.concatenate([own[at], other[at]], axis=1)


def first_kernel(own, other, part, ranks, far, rows, sem):
    role = lax.rem(lax.axis_index("par") + CHAIN, 2)
    copies = []

    def put(at, value):
        columns = slice(at, at + value.shape[1])
        rows[:, :, columns] = value.astype(BF).reshape(16, 32, value.shape[1])
        copies.append(pltpu.make_async_copy(rows.at[:, :, columns], part.at[:, :, columns], sem))
        copies[-1].start()

    def right(m):
        at = slice(DR + 128 * m, DR + 128 * m + 128)
        return jnp.concatenate([own[at], other[at]], axis=0)

    @pl.when(role == 0)
    def _():
        left = jnp.concatenate([own[UL:DR], other[UL:DR]], axis=1)
        for half in range(2):
            weight = left[128 * half : 128 * half + 128]
            low = lax.broadcasted_iota(jnp.int32, weight.shape, 0) < 64
            zero = jnp.zeros_like(weight)
            weight = [jnp.where(low, weight, zero), jnp.where(low, zero, weight)]
            grads = [rows_of(own, other, 2 + 2 * half + i) for i in range(2)]
            weight, grads = (jnp.concatenate(v, axis=1) for v in (weight, grads))
            put(512 + 128 * half, dot(grads, weight, 1, 1))
        hidden = rows_of(own, other, 0)
        put(0, dot(hidden, jnp.concatenate([right(0), right(1)], axis=1), 1, 0))
        put(256, dot(hidden, right(2), 1, 0))
        put(384, dot(rows_of(own, other, 1), right(3), 1, 0))
        for copy in copies:
            copy.wait()

    @pl.when(role == 1)
    def _():
        ends = [
            (own.at[pl.ds(RANKS, 64)], ranks.at[pl.ds(0, 64)]),
            (other.at[pl.ds(RANKS, 64)], ranks.at[pl.ds(64, 64)]),
            (other.at[pl.ds(0, UL)], far),
        ]
        moves = [pltpu.make_async_copy(a, b, sem) for a, b in ends]
        for move in moves:
            move.start()
        for move in moves:
            move.wait()


def first(own, other):
    shapes = [((16, 32, 768), BF), ((128, 128), BF), ((UL, 128), BF)]
    return call(
        first_kernel,
        shapes,
        own,
        other,
        scratch=[pltpu.VMEM((16, 32, 768), BF), pltpu.SemaphoreType.DMA],
        place=jax.ShapeDtypeStruct,
        out_specs=(HBM, HBM, HBM),
    )


ORDER = (0, 1, 3, 2)


def parts_kernel(gathered, up_right, down_left, *refs):
    inputs, (far, keep, send, for_a, for_b) = refs[:6], refs[6:]
    for m in range(4):
        for_a[m] = up_right[m].astype(F32)
    for half in range(2):
        for_b[half] = down_left[half].astype(F32).T
    z_hi = jnp.bitwise_and(lax.axis_index("ex"), 3)
    owners = [4 * y + jnp.bitwise_xor(z_hi, k) for y in range(4) for k in ORDER]
    owners = [pl.ds(pl.multiple_of(8 * owner, 8), 8) for owner in owners]
    nothing = jnp.zeros((8, 128), F32)
    left_half = lax.broadcasted_iota(jnp.int32, (256, 128), 1) < 64
    side = [[], []]
    for m in range(4):
        rows_a = [part for at in owners for part in (for_a[m, at, :], nothing)]
        rows_b = [part for at in owners for part in (nothing, for_b[m // 2, at, :])]
        rows_b = jnp.concatenate(rows_b, axis=0)
        rows_b = jnp.where(left_half if m % 2 == 0 else ~left_half, rows_b, 0.0)
        factor = jnp.concatenate([jnp.concatenate(rows_a, axis=0), rows_b], axis=1).astype(BF)
        for core in range(2):
            at = slice(64 * core + 16 * m, 64 * core + 16 * m + 16)
            ranks = gathered[:, at, :].reshape(256, 128)
            side[core].append(dot(ranks, factor, 0, 0).astype(BF))

    def weight(at, *modules):
        halves = [jnp.concatenate([half[m][:, at] for m in modules], axis=1) for half in side]
        return jnp.concatenate(halves, axis=0)

    def put(at, value):
        send[:, at : at + value.shape[1]] = value[:256].astype(BF)
        keep[:, at : at + value.shape[1]] = value[256:].astype(BF)

    x_at, g_at = slice(0, 128), slice(128, 256)
    def rows(k):
        return jnp.concatenate([inputs[k][...], far[512 * k : 512 * k + 512]], axis=1)

    hidden = rows(0)
    put(0, dot(hidden, weight(x_at, 0, 1), 1, 0))
    put(256, dot(hidden, weight(x_at, 2), 1, 0))
    put(384, dot(rows(1), weight(x_at, 3), 1, 0))
    for half in range(2):
        pair = jnp.concatenate([weight(g_at, 2 * half + i) for i in range(2)], axis=0)
        grads = jnp.concatenate([rows(2 + 2 * half + i) for i in range(2)], axis=1)
        put(512 + 128 * half, dot(grads, pair, 1, 0))


def parts(gathered, up_right, down_left, inputs, other):
    return call(
        parts_kernel,
        [((256, 768), BF)] * 2,
        gathered,
        up_right,
        down_left,
        *inputs,
        other,
        specs=[VMEM, LOOSE, LOOSE] + [VMEM] * 7,
        scratch=[pltpu.VMEM((4, 128, 128), F32), pltpu.VMEM((2, 128, 128), F32)],
        place=jax.ShapeDtypeStruct,
    )


def join_kernel(keep, got, out):
    def add_up(full, parts):
        for e in range(2):
            at = slice(128 * e, 128 * e + 128)
            total = jnp.zeros((64, 128), F32)
            for m in range(4):
                x, g = slice(128 * m, 128 * m + 128), slice(512 + 64 * m, 576 + 64 * m)
                total += dot(full[at, g], parts[at, x], 0, 0)
                total += dot(parts[at, g], full[at, x], 0, 0)
            out[:, 2 * e : 2 * e + 2] = total.reshape(32, 2, 128)

    mover = lax.rem(lax.axis_index("par"), 2) == CHAIN

    @pl.when(mover)
    def _():
        add_up(keep, got)

    @pl.when(jnp.logical_not(mover))
    def _():
        add_up(got, keep)


def move_rows(part, ranks, up_right, down_left, inputs, other):
    pieces = lax.all_to_all(part, "par", 0, 0, tiled=True, axis_index_groups=CHIPS)
    total = jnp.sum(pieces.astype(F32), axis=0).astype(BF)
    full = spread(total, "par", CHIPS).reshape(2, 256, 768)
    return full[0], full[1]


def swap(block, step):
    places = [(32 * e + p, 32 * (e ^ step) + p) for e in range(16) for p in range(1 - CHAIN, 32, 2)]
    return lax.ppermute(block, ("ex", "par"), places)


def gather_ranks(part, ranks, up_right, down_left, inputs, other):
    two = jnp.stack([ranks, swap(ranks, 1)])
    along_z = jnp.concatenate([two, swap(two, 3)]).reshape(512, 128)
    gathered = spread(along_z, "ex", Y).reshape(16, 128, 128)
    return parts(gathered, up_right, down_left, inputs, other)


def place_kernel(pieces, out):
    total = [pieces[core] for core in range(2)]
    for chip in range(1, 16):
        total = [total[core] + pieces[2 * chip + core] for core in range(2)]
    for e in range(4):
        rows = total[CHAIN if e < 2 else 1 - CHAIN] * (1.0 / 128)
        for i in range(2):
            at = 2 * (e % 2) + i
            out[e : e + 1, 128 * i : 128 * i + 128] = rows[at : at + 1]


def per_device(*args):
    inputs, (lora_a, lora_b, up_left, up_right, down_left, down_right) = args[:6], args[6:]

    down_left = down_left.transpose(0, 2, 1).reshape(2, 128, 128)
    own = pack(inputs, down_right, up_left, lora_a, lora_b)
    other = lax.ppermute(own, "par", PAIR)
    part, ranks, far = first(own, other)
    mover = lax.axis_index("par") % 2 == CHAIN
    rows = [a.reshape(512, 128) for a in inputs]
    operands = part, ranks, up_right, down_left, rows, far
    keep, send = lax.cond(mover, move_rows, gather_ranks, *operands)
    got = lax.ppermute(send, "par", PAIR)
    out = call(join_kernel, [((32, 4, 128), F32)], keep, got)[0]
    out = lax.all_to_all(out, "par", 0, 0, tiled=True)
    return call(place_kernel, [((4, 256), F32)], out, place=jax.ShapeDtypeStruct)[0]


def solution(mesh):
    in_specs = (P("ex", None, "par"),) * 6 + (
        P(None, "ex", "par"),
        P(None, "par", "ex"),
        P(None, "par", None),
        P(),
        P(),
        P(None, "par", None),
    )
    return jax.shard_map(
        per_device, mesh=mesh, in_specs=in_specs, out_specs=P("ex", "par"), check_vma=False
    )
```
